512 devices in a mesh: group: 16 (over x, z_hi), shard: 32 (over z_lo, y, core).
Axes of the slice: x: 4, y: 8, z: 8 (z_hi: 4, z_lo: 2; z = z_hi * 2 + z_lo), core: 2. Of those that a mesh axis runs over, the one named last changes fastest.
Arguments:
- user_shape: float32 [32768, 128], P(('group', 'shard')), may hold values from 1 to 10
- user_rate: float32 [32768, 128], P(('group', 'shard')), may hold values from 0.5 to 5
- item_shape: float32 [16384, 128], P('shard'), may hold values from 1 to 10
- item_rate: float32 [16384, 128], P('shard'), may hold values from 0.5 to 5
- tile_rows: int32 [65536], P(('group', 'shard')), may hold values from 0 to 15
- tile_cols: int32 [65536], P(('group', 'shard')), may hold values from 0 to 3
- clicks: bfloat16 [65536, 128, 128], P(('group', 'shard')), may hold values from 0 to 5, as said below
- tile_count: int32 [512], P(('group', 'shard')), may hold values from 16 to 128, as said below
Outputs:
- user_shape_new: float32 [32768, 128], P(('group', 'shard'))
- item_shape_new: float32 [16384, 128], P('shard')
The draws below stay inside these ranges and needn't reach their ends.
Inputs may be any that keep to these rules, and one draw needn't show every extreme that they name: `clicks`: every count is a whole number 0 to 5; most are 0. `tile_count`: some device has all 128 slots live in every draw; a device's block pairs may repeat.
All inputs are finite; a program needn't handle non-finite values.
Results may differ from the reference program's by a relative error of at most 0.0028.
Values may be sent and summed in bfloat16 or wider, within the bound.
No kernel may reach another device: no remote copies, remote signals or barrier semaphores. Data moves between devices by JAX's collectives and lax.ppermute only.
A program may use at most 64 MiB of HBM per device.

```python
import math
import jax
import jax.numpy as jnp
from jax import lax

COMPONENTS = 128
TILE = 128
I_DEV = 512
TILE_CAP = 128
GROUP_USERS = 2048
USER_BLOCKS = 16
ITEM_BLOCKS = 4
USERS = 32768
ITEMS = 16384
TILES = 65536
N_SHARD = 32


def draw_clicks(key, part):
    raw = jax.random.randint(key, (TILES, TILE, TILE), 0, 64, dtype=jnp.int32)
    counts = jnp.maximum(raw - 58, 0).at[0, 0, 0].set(5)
    return counts.astype(jnp.float32).astype(jnp.bfloat16)


def draw_tile_count(key, part):
    devices = TILES // TILE_CAP
    lowest = max(TILE_CAP // 8, 1)
    base = jax.random.randint(key, (devices,), lowest, TILE_CAP + 1, dtype=jnp.int32)
    where_full = jax.random.randint(jax.random.fold_in(key, 3), (), 0, devices, dtype=jnp.int32)
    where_low = (where_full + 1) % devices
    return base.at[where_full].set(TILE_CAP).at[where_low].set(lowest)


def touch_ends(entries, rng, least, largest):
    spot = [jax.random.randint(jax.random.fold_in(rng, axis), (), 0, length) for axis, length in enumerate(entries.shape)]
    main_axis = entries.shape.index(max(entries.shape))
    beside = spot[:main_axis] + [(spot[main_axis] + 1) % entries.shape[main_axis]] + spot[main_axis + 1:]
    return entries.at[tuple(spot)].set(least).at[tuple(beside)].set(largest)


def level_of(stream_key, dims, pieces, least, high):
    gain, own = 1.0, jax.random.fold_in(stream_key, 6)
    for axis_at, blocks in pieces:
        steps = jnp.exp(jax.random.uniform(jax.random.fold_in(own, axis_at), (blocks,), jnp.float32, least / len(pieces), high / len(pieces)))
        gain = gain * jnp.repeat(steps, dims[axis_at] // blocks).reshape([-1 if axis == axis_at else 1 for axis in range(len(dims))])
    return gain


def setup_inputs(seed: int = 0) -> dict:
    streams_of = jax.random.split(jax.random.key(seed), 9)
    user_shape = jnp.clip(jnp.exp(math.log(10.0) - 2.3025851 * jax.random.uniform(streams_of[0], (USERS, COMPONENTS), jnp.float32) ** level_of(streams_of[0], (USERS, COMPONENTS), ((0, 512),), -0.2, 0.2)), 1.0, 10.0)
    user_rate = jnp.clip(jnp.exp(math.log(5.0) - 2.3025851 * jax.random.uniform(streams_of[1], (USERS, COMPONENTS), jnp.float32) ** level_of(streams_of[1], (USERS, COMPONENTS), ((0, 512),), -0.2, 0.2)), 0.5, 5.0)
    item_shape = jnp.clip(jnp.exp(math.log(10.0) - 2.3025851 * jax.random.uniform(streams_of[2], (ITEMS, COMPONENTS), jnp.float32) ** level_of(streams_of[2], (ITEMS, COMPONENTS), ((0, 32),), -0.2, 0.2)), 1.0, 10.0)
    item_rate = jnp.clip(jnp.exp(math.log(5.0) - 2.3025851 * jax.random.uniform(streams_of[3], (ITEMS, COMPONENTS), jnp.float32) ** level_of(streams_of[3], (ITEMS, COMPONENTS), ((0, 32),), -0.2, 0.2)), 0.5, 5.0)
    tile_rows = touch_ends(jax.random.randint(streams_of[4], (TILES,), 0, USER_BLOCKS), jax.random.fold_in(streams_of[4], 1), 0, USER_BLOCKS - 1).astype(jnp.int32)
    tile_cols = touch_ends(jax.random.randint(streams_of[5], (TILES,), 0, ITEM_BLOCKS), jax.random.fold_in(streams_of[5], 1), 0, ITEM_BLOCKS - 1).astype(jnp.int32)
    clicks = draw_clicks(jax.random.fold_in(streams_of[8], 71), 0)
    tile_count = draw_tile_count(jax.random.fold_in(streams_of[8], 71), 0)
    return {"user_shape": user_shape, "user_rate": user_rate, "item_shape": item_shape, "item_rate": item_rate, "tile_rows": tile_rows, "tile_cols": tile_cols, "clicks": clicks, "tile_count": tile_count}


prior_shape = 0.3


def factors(shape, rate):
    return jnp.exp(lax.digamma(shape) - jnp.log(rate)).astype(jnp.bfloat16)


def reference(user_shape, user_rate, item_shape, item_rate, tile_rows, tile_cols, clicks, tile_count):
    user_factor = factors(user_shape, user_rate)
    item_factor = factors(item_shape, item_rate)
    devices = tile_count.shape[0]
    slots = tile_rows.shape[0]
    capacity = slots // devices
    edge = clicks.shape[1]
    slot_index = jnp.arange(slots, dtype=jnp.int32)
    device = slot_index // capacity
    live = ((slot_index % capacity) < tile_count[device]).astype(jnp.float32)
    group_index = device // N_SHARD
    shard_index = device % N_SHARD
    user_start = (group_index * GROUP_USERS + tile_rows * edge).astype(jnp.int32)
    item_start = (shard_index * I_DEV + tile_cols * edge).astype(jnp.int32)

    def step(carry, inputs):
        user_acc, item_acc = carry
        ustart, istart, counts, weight = inputs
        a = lax.dynamic_slice_in_dim(user_factor, ustart, edge, 0)
        b = lax.dynamic_slice_in_dim(item_factor, istart, edge, 0)
        denom = jnp.dot(a, b.T, preferred_element_type=jnp.float32)
        ratio = (counts.astype(jnp.float32) * weight / denom).astype(jnp.bfloat16)
        user_add = a.astype(jnp.float32) * jnp.dot(ratio, b, preferred_element_type=jnp.float32)
        item_add = b.astype(jnp.float32) * jnp.dot(ratio.T, a, preferred_element_type=jnp.float32)
        old_user = lax.dynamic_slice_in_dim(user_acc, ustart, edge, 0)
        user_acc = lax.dynamic_update_slice_in_dim(user_acc, old_user + user_add, ustart, 0)
        old_item = lax.dynamic_slice_in_dim(item_acc, istart, edge, 0)
        item_acc = lax.dynamic_update_slice_in_dim(item_acc, old_item + item_add, istart, 0)
        return (user_acc, item_acc), None

    start = (jnp.zeros(user_shape.shape, jnp.float32), jnp.zeros(item_shape.shape, jnp.float32))
    (user_acc, item_acc), _ = lax.scan(step, start, (user_start, item_start, clicks, live))
    return prior_shape + user_acc, prior_shape + item_acc
```

```python
import functools
import jax
import jax.numpy as jnp
from jax import lax
from jax.experimental import pallas as pl
from jax.experimental.pallas import tpu as pltpu
from jax.sharding import PartitionSpec as P

CHUNK = 16
STEP = 4

prior_shape = 0.3
f32 = jnp.float32
bf16 = jnp.bfloat16


def factors(shape, rate):
    return jnp.exp(lax.digamma(shape) - jnp.log(rate)).astype(bf16)


def add_clicks(slots, edge, rows_ref, cols_ref, count_ref, clicks_ref, out_ref, done_ref, total, held, sems):
    chunks = slots // CHUNK
    count = count_ref[0]

    def copy(c):
        part = pl.ds(c * CHUNK, CHUNK)
        return pltpu.make_async_copy(clicks_ref.at[part], held.at[part], sems.at[c])

    for c in range(chunks):
        @pl.when(c * CHUNK < count)
        def _():
            copy(c).start()

    def clear(r, carry):
        total[r] = jnp.zeros(total.shape[1:], f32)
        return carry

    lax.fori_loop(0, total.shape[0], clear, 0)

    def add(t, carry):
        row = rows_ref[t]
        cols = pl.ds(pl.multiple_of(cols_ref[t] * edge, edge), edge)
        total[row, :, cols] += held[t].astype(f32)
        return carry

    for c in range(chunks):
        @pl.when(c * CHUNK < count)
        def _():
            copy(c).wait()
            lax.fori_loop(c * CHUNK, jnp.minimum(count, (c + 1) * CHUNK), add, 0)

    def finish(r, carry):
        out_ref[r] = total[r].astype(bf16)
        return carry

    lax.fori_loop(0, total.shape[0], finish, 0)
    done_ref[...] = jnp.zeros_like(done_ref)


def pair_clicks(tile_rows, tile_cols, tile_count, clicks, user_blocks, item_blocks):
    slots, edge, _ = clicks.shape
    smem = pl.BlockSpec(memory_space=pltpu.SMEM)
    return pl.pallas_call(
        functools.partial(add_clicks, slots, edge),
        out_shape=(
            pltpu.VMEM((user_blocks, edge, item_blocks * edge), bf16),
            pltpu.VMEM((8, 128), f32),
        ),
        in_specs=[smem, smem, smem, pl.BlockSpec(memory_space=pltpu.HBM)],
        out_specs=(pl.BlockSpec(memory_space=pltpu.VMEM),) * 2,
        scratch_shapes=[
            pltpu.VMEM((user_blocks, edge, item_blocks * edge), f32),
            pltpu.VMEM((slots, edge, edge), bf16),
            pltpu.SemaphoreType.DMA((slots // CHUNK,)),
        ],
        compiler_params=pltpu.CompilerParams(vmem_limit_bytes=56 << 20),
        cost_estimate=pl.CostEstimate(flops=slots * edge * edge, bytes_accessed=2 * slots * edge * edge, transcendentals=0),
        name="pair_clicks",
    )(tile_rows, tile_cols, tile_count, clicks)


def half_terms(start_ref, a_ref, b_ref, counts_ref, user_ref, item_ref, total):
    blocks, half, comps = a_ref.shape
    rows = STEP * half
    first = pl.multiple_of(start_ref[0], half)
    b = b_ref[...]
    total[...] = jnp.zeros_like(total)

    def step(i, carry):
        at = pl.ds(i * STEP, STEP)
        a = a_ref[at].reshape(rows, comps)
        counts = counts_ref[at, pl.ds(first, half), :].reshape(rows, -1)
        denom = lax.dot_general(a, b, (((1,), (1,)), ((), ())), preferred_element_type=f32)
        ratio = (counts.astype(f32) / denom).astype(bf16)
        product = jnp.dot(ratio, b, preferred_element_type=f32)
        terms = a.astype(f32) * product
        user_ref[at] = terms.reshape(STEP, half, comps).astype(user_ref.dtype)
        total[...] += lax.dot_general(a, ratio, (((0,), (0,)), ((), ())), preferred_element_type=f32)
        return carry

    lax.fori_loop(0, blocks // STEP, step, 0)


def first_half(start_ref, a_ref, b_ref, counts_ref, done_ref, user_ref, item_ref, total):
    half_terms(start_ref, a_ref, b_ref, counts_ref, user_ref, item_ref, total)
    item_ref[...] = total[...]


def second_half(start_ref, a_ref, b_ref, counts_ref, before_ref, user_ref, item_ref, total):
    half_terms(start_ref, a_ref, b_ref, counts_ref, user_ref, item_ref, total)
    both = (before_ref[...] + total[...]).T
    item_ref[...] = (b_ref[...].astype(f32) * both).astype(item_ref.dtype)


def join_cores(z_ref, mine_ref, got_ref, keep_ref, send_ref):
    blocks = keep_ref.shape[0]
    kept = pl.ds(z_ref[0] * blocks, blocks)
    sent = pl.ds((1 - z_ref[0]) * blocks, blocks)
    keep_ref[...] = mine_ref[kept] + got_ref[kept].astype(f32)
    send_ref[...] = (mine_ref[sent] + got_ref[sent].astype(f32)).astype(bf16)


def join_chips(keep_ref, got_ref, out_ref):
    out_ref[...] = (keep_ref[...] + got_ref[...].astype(f32)).astype(bf16)


def sum_items(parts_ref, after_ref, out_ref):
    total = jnp.sum(parts_ref[...].astype(f32), 0)
    out_ref[...] = jnp.broadcast_to(total.astype(bf16)[None], out_ref.shape)


def sum_users(parts_ref, out_ref):
    out_ref[...] = prior_shape + jnp.sum(parts_ref[...].astype(f32), 0)


def small(kernel, name, out_shape, *operands, specs=None):
    vmem = pl.BlockSpec(memory_space=pltpu.VMEM)
    return pl.pallas_call(
        kernel,
        out_shape=out_shape,
        in_specs=specs or [vmem] * len(operands),
        out_specs=jax.tree.map(lambda _: vmem, out_shape),
        compiler_params=pltpu.CompilerParams(vmem_limit_bytes=8 << 20),
        name=name,
    )(*operands)


def run_half(kernel, name, start, a, b, counts, extra, user_type, item_shape, item_type):
    vmem = pl.BlockSpec(memory_space=pltpu.VMEM)
    blocks, half, comps = a.shape
    items = b.shape[0]
    return pl.pallas_call(
        kernel,
        out_shape=(
            pltpu.VMEM(a.shape, user_type),
            pltpu.VMEM(item_shape, item_type),
        ),
        in_specs=[pl.BlockSpec(memory_space=pltpu.SMEM)] + [vmem] * (3 + len(extra)),
        out_specs=(vmem, vmem),
        scratch_shapes=[pltpu.VMEM((comps, items), f32)],
        compiler_params=pltpu.CompilerParams(vmem_limit_bytes=16 << 20),
        cost_estimate=pl.CostEstimate(flops=6 * blocks * half * comps * items, bytes_accessed=4 * blocks * half * items, transcendentals=0),
        name=name,
    )(start, a, b, counts, *extra)


def body(n_group, n_shard, user_shape, user_rate, item_shape, item_rate, tile_rows, tile_cols, clicks, tile_count):
    own, comps = user_shape.shape
    items = item_shape.shape[0]
    edge = clicks.shape[1]
    chips = n_shard // 2
    swap = [(s, s ^ 1) for s in range(n_shard)]
    cross = [(s, s ^ chips) for s in range(n_shard)]
    same_core = [[2 * r + c for r in range(chips)] for c in range(2)]
    along_y = [[z * chips + 2 * y + c for y in range(chips // 2)] for z in range(2) for c in range(2)]
    place = lax.axis_index("shard")
    core = place & 1
    z = (place // chips).astype(jnp.int32).reshape(1)
    start = (core * own).astype(jnp.int32).reshape(1)

    def exchange(x):
        return lax.all_to_all(x, "shard", 0, 0, axis_index_groups=same_core)

    user_local = factors(user_shape, user_rate)
    a_mine = exchange(jnp.broadcast_to(user_local[None], (chips, own, comps)))
    b = factors(item_shape, item_rate)
    counts, done = pair_clicks(tile_rows, tile_cols, tile_count, clicks, chips, items // edge)
    a_mine, b, done = lax.optimization_barrier((a_mine, b, done))
    a_other = lax.ppermute(a_mine, "shard", swap)
    user_mine, item_part = run_half(first_half, "first_half", start, a_mine, b, counts, (done,), f32, (comps, items), f32)
    user_other, item_sum = run_half(second_half, "second_half", own - start, a_other, b, counts, (item_part,), bf16, (items, comps), bf16)

    user_sent = lax.ppermute(user_other, "shard", swap)
    item_parts = lax.all_to_all(item_sum.reshape(n_group, items // n_group, comps), "group", 0, 0)
    quarter = (chips // 2, own, comps)
    smem, vmem = pl.BlockSpec(memory_space=pltpu.SMEM), pl.BlockSpec(memory_space=pltpu.VMEM)
    keep, send = small(
        join_cores, "join_cores", (pltpu.VMEM(quarter, f32), pltpu.VMEM(quarter, bf16)), z, user_mine, user_sent,
        specs=[smem, vmem, vmem],
    )
    got = lax.ppermute(send, "shard", cross)
    item_piece = small(
        sum_items, "sum_items", jax.ShapeDtypeStruct(item_parts.shape, bf16), item_parts, send,
        specs=[vmem, pl.BlockSpec(memory_space=pl.ANY)],
    )
    item_all = lax.all_to_all(item_piece, "group", 0, 0)
    user_quad = small(join_chips, "join_chips", jax.ShapeDtypeStruct(quarter, bf16), keep, got)
    user_quad, item_all = lax.optimization_barrier((user_quad, item_all))
    user_parts = lax.all_to_all(user_quad, "shard", 0, 0, axis_index_groups=along_y)
    user_new = small(sum_users, "sum_users", jax.ShapeDtypeStruct((own, comps), f32), user_parts)
    item_new = prior_shape + item_all.reshape(items, comps).astype(f32)
    return user_new, item_new


def solution(mesh):
    return jax.shard_map(
        functools.partial(body, mesh.shape["group"], mesh.shape["shard"]),
        mesh=mesh,
        in_specs=(
            P(("group", "shard"), None),
            P(("group", "shard"), None),
            P("shard", None),
            P("shard", None),
            P(("group", "shard")),
            P(("group", "shard")),
            P(("group", "shard"), None, None),
            P(("group", "shard")),
        ),
        out_specs=(P(("group", "shard"), None), P("shard", None)),
        check_vma=False,
    )
```

```python
import functools
import jax
import jax.numpy as jnp
from jax import lax
from jax.experimental import pallas as pl
from jax.experimental.pallas import tpu as pltpu
from jax.sharding import PartitionSpec as P

CHUNK = 16
STEP = 4

prior_shape = 0.3
f32 = jnp.float32
bf16 = jnp.bfloat16
ROWS = (((0,), (0,)), ((), ()))
LANES = (((1,), (1,)), ((), ()))


def factors(shape, rate):
    y = shape + 6.0
    u = shape * (shape + 5.0)
    below = (2.0 * shape + 5.0) * ((3.0 * u + 20.0) * u + 24.0) / (u * ((u + 10.0) * u + 24.0))
    w = 1.0 / y
    v = w * w
    tail = 0.5 * w + v * (1.0 / 12.0 - v * (1.0 / 120.0 - v * (1.0 / 252.0)))
    return (y / rate * jnp.exp(-(tail + below))).astype(bf16)


def user_copies(shape_ref, rate_ref, out_ref):
    out_ref[...] = jnp.broadcast_to(factors(shape_ref[...], rate_ref[...])[None], out_ref.shape)


def add_clicks(slots, edge, core_ref, rows_ref, cols_ref, count_ref, clicks_ref, shape_ref, rate_ref, kept_ref, sent_ref, factors_ref, total, held, sems):
    chunks = slots // CHUNK
    count = count_ref[0]
    blocks, _, items = total.shape
    half = kept_ref.shape[1]

    def copy(c):
        part = pl.ds(c * CHUNK, CHUNK)
        return pltpu.make_async_copy(clicks_ref.at[part], held.at[part], sems.at[c])

    for c in range(chunks):
        @pl.when(c * CHUNK < count)
        def _():
            copy(c).start()

    def clear(r, carry):
        total[r] = jnp.zeros(total.shape[1:], f32)
        return carry

    lax.fori_loop(0, blocks, clear, 0)
    wide = items // factors_ref.shape[1]
    for j in range(items // half):
        part = slice(j * half, (j + 1) * half)
        lanes = slice(j % wide * edge, (j % wide + 1) * edge)
        b = factors(shape_ref[part], rate_ref[part])
        factors_ref[part] = b
        sent_ref[blocks + j // wide, :, lanes] = b

    def add(t, carry):
        row = rows_ref[t]
        cols = pl.ds(pl.multiple_of(cols_ref[t] * edge, edge), edge)
        total[row, :, cols] += held[t].astype(f32)
        return carry

    for c in range(chunks):
        @pl.when(c * CHUNK < count)
        def _():
            copy(c).wait()
            lax.fori_loop(c * CHUNK, jnp.minimum(count, (c + 1) * CHUNK), add, 0)

    first = core_ref[0] * half
    kept = pl.ds(pl.multiple_of(first, half), half)
    sent = pl.ds(pl.multiple_of(half - first, half), half)

    def finish(r, carry):
        kept_ref[r] = total[r, kept, :].astype(bf16)
        sent_ref[r] = total[r, sent, :].astype(bf16)
        return carry

    lax.fori_loop(0, blocks, finish, 0)


def pair_clicks(core, tile_rows, tile_cols, tile_count, clicks, item_shape, item_rate, blocks):
    slots, edge, _ = clicks.shape
    items, comps = item_shape.shape
    half = edge // 2
    smem, vmem = pl.BlockSpec(memory_space=pltpu.SMEM), pl.BlockSpec(memory_space=pltpu.VMEM)
    return pl.pallas_call(
        functools.partial(add_clicks, slots, edge),
        out_shape=(
            pltpu.VMEM((blocks, half, items), bf16),
            pltpu.VMEM((blocks + comps // half, half, items), bf16),
            pltpu.VMEM((items, comps), bf16),
        ),
        in_specs=[smem] * 4 + [pl.BlockSpec(memory_space=pltpu.HBM), vmem, vmem],
        out_specs=(vmem,) * 3,
        scratch_shapes=[
            pltpu.VMEM((blocks, edge, items), f32),
            pltpu.VMEM((slots, edge, edge), bf16),
            pltpu.SemaphoreType.DMA((slots // CHUNK,)),
        ],
        compiler_params=pltpu.CompilerParams(vmem_limit_bytes=56 << 20),
        cost_estimate=pl.CostEstimate(flops=slots * edge * edge, bytes_accessed=2 * slots * edge * edge, transcendentals=0),
        name="pair_clicks",
    )(core, tile_rows, tile_cols, tile_count, clicks, item_shape, item_rate)


def add_terms(a_ref, counts_ref, b, add_users, total):
    blocks, half, comps = a_ref.shape
    rows = STEP * half
    total[...] = jnp.zeros_like(total)

    def step(i, carry):
        at = pl.ds(i * STEP, STEP)
        a = a_ref[at].reshape(rows, comps)
        denom = lax.dot_general(a, b, LANES, preferred_element_type=f32)
        ratio = (counts_ref[at].reshape(rows, -1).astype(f32) / denom).astype(bf16)
        product = jnp.dot(ratio, b, preferred_element_type=f32)
        add_users(at, (a.astype(f32) * product).reshape(STEP, half, comps))
        total[...] += lax.dot_general(a, ratio, ROWS, preferred_element_type=f32)
        return carry

    lax.fori_loop(0, blocks // STEP, step, 0)


def place_items(b, sums, out_ref, part, items_of):
    blocks = out_ref.shape[0]
    terms = (b.astype(f32) * sums.T).reshape(blocks, items_of, -1)
    out_ref[:, pl.ds(pl.multiple_of(part * items_of, items_of), items_of), :] = terms


def own_items(core_ref, a_ref, counts_ref, b_ref, user_ref, item_ref, total):
    b = b_ref[...]

    def add_users(at, terms):
        user_ref[at] = terms

    add_terms(a_ref, counts_ref, b, add_users, total)
    place_items(b, total[...], item_ref, core_ref[0], b.shape[0] // item_ref.shape[0])


def other_items(core_ref, a_ref, got_ref, user_ref, item_ref, keep_ref, send_ref, total, users, items):
    core = core_ref[0]
    blocks, half, comps = a_ref.shape
    b = jnp.concatenate(
        [
            got_ref[blocks + q, :, j : j + comps]
            for q in range(comps // half)
            for j in range(0, got_ref.shape[2], comps)
        ],
        0,
    )

    def add_users(at, terms):
        users[at] = user_ref[at] + terms

    add_terms(a_ref, got_ref, b, add_users, total)
    rows = b.shape[0] // blocks
    items[...] = item_ref[...]
    place_items(b, total[...], items, 1 - core, rows)

    @pl.when(core == 0)
    def _():
        keep_ref[...] = users[...]
        send_ref[...] = items[...].astype(bf16)

    @pl.when(core != 0)
    def _():
        keep_ref[...] = items[...]
        send_ref[...] = users[...].astype(bf16)


def assemble(core_ref, keep_ref, got_ref, out_ref):
    half = keep_ref.shape[1]

    @pl.when(core_ref[0] == 0)
    def _():
        out_ref[:, :half] = keep_ref[...].astype(bf16)
        out_ref[:, half:] = got_ref[...]

    @pl.when(core_ref[0] != 0)
    def _():
        total = keep_ref[...] + got_ref[...].astype(f32)
        rounded = total.astype(bf16)
        out_ref[:, :half] = rounded
        out_ref[:, half:] = (total - rounded.astype(f32)).astype(bf16)


def join(parts_ref, keep_ref, send_ref, items_ref):
    total = jnp.sum(parts_ref[...].astype(f32), 0)
    half = total.shape[0] // 2
    keep_ref[...] = prior_shape + total[:half]
    send_ref[...] = prior_shape + total[half:]
    pieces = (total[:half] + total[half:]).astype(bf16).reshape((2,) + items_ref.shape[2:])
    items_ref[...] = jnp.broadcast_to(pieces[None], items_ref.shape)


def small(kernel, out_shape, *operands, core=None, scratch=(), cost=None):
    vmem = pl.BlockSpec(memory_space=pltpu.VMEM)
    lead = () if core is None else (core,)
    return pl.pallas_call(
        kernel,
        out_shape=out_shape,
        in_specs=[pl.BlockSpec(memory_space=pltpu.SMEM)] * len(lead) + [vmem] * len(operands),
        out_specs=jax.tree.map(lambda _: vmem, out_shape),
        scratch_shapes=list(scratch),
        compiler_params=pltpu.CompilerParams(vmem_limit_bytes=24 << 20),
        cost_estimate=cost,
        name=kernel.__name__,
    )(*lead, *operands)


def body(n_group, n_shard, user_shape, user_rate, item_shape, item_rate, tile_rows, tile_cols, clicks, tile_count):
    own, comps = user_shape.shape
    items = item_shape.shape[0]
    edge = clicks.shape[1]
    chips = n_shard // 2
    both = ("group", "shard")
    swap = [(s, s ^ 1) for s in range(n_shard)]
    same_core = [[2 * r + c for r in range(chips)] for c in range(2)]
    users_or_items = [[g * n_shard + 2 * r for r in range(chips)] for g in range(n_group)]
    users_or_items += [[g * n_shard + 2 * r + 1 for g in range(n_group)] for r in range(chips)]
    same_chip = [[g * n_shard + 2 * r + c for g in range(n_group) for c in range(2)] for r in range(chips)]
    core = (lax.axis_index("shard") & 1).astype(jnp.int32).reshape(1)

    copies = small(user_copies, jax.ShapeDtypeStruct((chips, own, comps), bf16), user_shape, user_rate)
    a_mine = lax.all_to_all(copies, "shard", 0, 0, axis_index_groups=same_core)
    kept, sent, b = pair_clicks(core, tile_rows, tile_cols, tile_count, clicks, item_shape, item_rate, chips)
    other = lax.ppermute(sent, "shard", swap)
    whole = (chips, own, comps)
    total = pltpu.VMEM((comps, items), f32)
    cost = pl.CostEstimate(flops=1 << 34, bytes_accessed=1 << 24, transcendentals=0)
    users, item_sums = small(own_items, (pltpu.VMEM(whole, f32), pltpu.VMEM(whole, f32)), a_mine, kept, b, core=core, scratch=(total,), cost=cost)
    keep, send = small(
        other_items, (pltpu.VMEM(whole, f32), pltpu.VMEM(whole, bf16)), a_mine, other, users, item_sums,
        core=core, scratch=(total, pltpu.VMEM(whole, f32), pltpu.VMEM(whole, f32)),
    )
    got = lax.ppermute(send, "shard", swap)
    terms = small(assemble, jax.ShapeDtypeStruct((chips, edge, comps), bf16), keep, got, core=core)
    parts = lax.all_to_all(terms, both, 0, 0, axis_index_groups=users_or_items)
    piece = (2, items // n_group, comps)
    keep, send, pieces = small(
        join,
        (
            jax.ShapeDtypeStruct((own, comps), f32),
            jax.ShapeDtypeStruct((own, comps), f32),
            jax.ShapeDtypeStruct((n_group,) + piece, bf16),
        ),
        parts,
    )
    item_all = lax.all_to_all(pieces.reshape((2 * n_group,) + piece[1:]), both, 0, 0, axis_index_groups=same_chip)
    got = lax.ppermute(send, "shard", swap)
    user_new = jnp.where(core[0] == 0, keep, got)
    item_new = prior_shape + item_all.reshape((n_group,) + piece)[:, 1].reshape(items, comps).astype(f32)
    return user_new, item_new


def solution(mesh):
    return jax.shard_map(
        functools.partial(body, mesh.shape["group"], mesh.shape["shard"]),
        mesh=mesh,
        in_specs=(
            P(("group", "shard"), None),
            P(("group", "shard"), None),
            P("shard", None),
            P("shard", None),
            P(("group", "shard")),
            P(("group", "shard")),
            P(("group", "shard"), None, None),
            P(("group", "shard")),
        ),
        out_specs=(P(("group", "shard"), None), P("shard", None)),
        check_vma=False,
    )
```

```python
import functools
import jax
import jax.numpy as jnp
from jax import lax
from jax.experimental import pallas as pl
from jax.experimental.pallas import tpu as pltpu
from jax.sharding import PartitionSpec as P

CHUNK = 16
STEP = 4

prior_shape = 0.3
f32 = jnp.float32
bf16 = jnp.bfloat16
ROWS = (((0,), (0,)), ((), ()))
LANES = (((1,), (1,)), ((), ()))


def factors(shape, rate):
    y = shape + 6.0
    u = shape * (shape + 5.0)
    below = (2.0 * shape + 5.0) * ((3.0 * u + 20.0) * u + 24.0) / (u * ((u + 10.0) * u + 24.0))
    w = 1.0 / y
    v = w * w
    tail = 0.5 * w + v * (1.0 / 12.0 - v * (1.0 / 120.0 - v * (1.0 / 252.0)))
    return (y / rate * jnp.exp(-(tail + below))).astype(bf16)


def user_copies(shape_ref, rate_ref, out_ref):
    out_ref[...] = jnp.broadcast_to(factors(shape_ref[...], rate_ref[...])[None], out_ref.shape)


def add_clicks(slots, edge, core_ref, rows_ref, cols_ref, count_ref, clicks_ref, shape_ref, rate_ref, kept_ref, tail_ref, sent_ref, total, held, staged, sems):
    chunks = slots // CHUNK
    count = count_ref[0]
    blocks, _, items = total.shape
    half = staged.shape[1]
    near = kept_ref.shape[0]

    def copy(c):
        part = pl.ds(c * CHUNK, CHUNK)
        return pltpu.make_async_copy(clicks_ref.at[part], held.at[part], sems.at[c])

    for c in range(chunks):
        @pl.when(c * CHUNK < count)
        def _():
            copy(c).start()

    def clear(r, carry):
        total[r] = jnp.zeros(total.shape[1:], f32)
        return carry

    lax.fori_loop(0, blocks, clear, 0)
    wide = items // edge
    for j in range(items // half):
        part = slice(j * half, (j + 1) * half)
        lanes = slice(j % wide * edge, (j % wide + 1) * edge)
        sent_ref[blocks + j // wide, :, lanes] = factors(shape_ref[part], rate_ref[part])

    def add(t, carry):
        row = rows_ref[t]
        cols = pl.ds(pl.multiple_of(cols_ref[t] * edge, edge), edge)
        total[row, :, cols] += held[t].astype(f32)
        return carry

    for c in range(chunks):
        @pl.when(c * CHUNK < count)
        def _():
            copy(c).wait()
            lax.fori_loop(c * CHUNK, jnp.minimum(count, (c + 1) * CHUNK), add, 0)

    first = core_ref[0] * half
    kept = pl.ds(pl.multiple_of(first, half), half)
    sent = pl.ds(pl.multiple_of(half - first, half), half)

    def keep_tail(r, carry):
        staged[r] = total[near + r, kept, :].astype(bf16)
        return carry

    def keep(r, carry):
        kept_ref[r] = total[r, kept, :].astype(bf16)
        return carry

    def send(r, carry):
        sent_ref[r] = total[r, sent, :].astype(bf16)
        return carry

    lax.fori_loop(0, blocks - near, keep_tail, 0)
    out = pltpu.make_async_copy(staged, tail_ref, sems.at[chunks])
    out.start()
    lax.fori_loop(0, near, keep, 0)
    lax.fori_loop(0, blocks, send, 0)
    out.wait()


def pair_clicks(core, tile_rows, tile_cols, tile_count, clicks, item_shape, item_rate, blocks):
    slots, edge, _ = clicks.shape
    items, comps = item_shape.shape
    half = edge // 2
    smem, vmem = pl.BlockSpec(memory_space=pltpu.SMEM), pl.BlockSpec(memory_space=pltpu.VMEM)
    return pl.pallas_call(
        functools.partial(add_clicks, slots, edge),
        out_shape=(
            pltpu.VMEM((blocks - STEP, half, items), bf16),
            pltpu.HBM((STEP, half, items), bf16),
            pltpu.VMEM((blocks + comps // half, half, items), bf16),
        ),
        in_specs=[smem] * 4 + [pl.BlockSpec(memory_space=pltpu.HBM), vmem, vmem],
        out_specs=(vmem, pl.BlockSpec(memory_space=pltpu.HBM), vmem),
        scratch_shapes=[
            pltpu.VMEM((blocks, edge, items), f32),
            pltpu.VMEM((slots, edge, edge), bf16),
            pltpu.VMEM((STEP, half, items), bf16),
            pltpu.SemaphoreType.DMA((slots // CHUNK + 1,)),
        ],
        compiler_params=pltpu.CompilerParams(vmem_limit_bytes=56 << 20),
        cost_estimate=pl.CostEstimate(flops=slots * edge * edge, bytes_accessed=2 * slots * edge * edge, transcendentals=0),
        name="pair_clicks",
    )(core, tile_rows, tile_cols, tile_count, clicks, item_shape, item_rate)


def sent_factors(sent_ref, blocks, comps):
    return jnp.concatenate(
        [sent_ref[q, :, j : j + comps] for q in range(blocks, sent_ref.shape[0]) for j in range(0, sent_ref.shape[2], comps)],
        0,
    )


def add_terms(a_ref, counts_of, b, add_users, total):
    blocks, half, comps = a_ref.shape
    rows = STEP * half
    total[...] = jnp.zeros_like(total)
    for i in range(blocks // STEP):
        at = pl.ds(i * STEP, STEP)
        a = a_ref[at].reshape(rows, comps)
        denom = lax.dot_general(a, b, LANES, preferred_element_type=f32)
        ratio = (counts_of(i).reshape(rows, -1).astype(f32) / denom).astype(bf16)
        product = jnp.dot(ratio, b, preferred_element_type=f32)
        add_users(at, (a.astype(f32) * product).reshape(STEP, half, comps))
        total[...] += lax.dot_general(a, ratio, ROWS, preferred_element_type=f32)


def place_items(b, sums, out_ref, part, items_of):
    blocks = out_ref.shape[0]
    terms = (b.astype(f32) * sums.T).reshape(blocks, items_of, -1)
    out_ref[:, pl.ds(pl.multiple_of(part * items_of, items_of), items_of), :] = terms


def own_items(core_ref, a_ref, sent_ref, kept_ref, tail_ref, user_ref, item_ref, same_ref, total, held, sem):
    blocks, _, comps = a_ref.shape
    copy = pltpu.make_async_copy(tail_ref, held, sem)
    copy.start()
    b = sent_factors(sent_ref, blocks, comps)

    def counts_of(i):
        if (i + 1) * STEP <= kept_ref.shape[0]:
            return kept_ref[i * STEP : (i + 1) * STEP]
        copy.wait()
        return held[...]

    def add_users(at, terms):
        user_ref[at] = terms

    add_terms(a_ref, counts_of, b, add_users, total)
    place_items(b, total[...], item_ref, core_ref[0], b.shape[0] // blocks)


def near_items(core, a, sent, kept, tail):
    smem, vmem, hbm = (pl.BlockSpec(memory_space=m) for m in (pltpu.SMEM, pltpu.VMEM, pltpu.HBM))
    items = sent.shape[2]
    users, item_sums, _ = pl.pallas_call(
        own_items,
        out_shape=(pltpu.VMEM(a.shape, f32), pltpu.VMEM(a.shape, f32), pltpu.HBM(tail.shape, bf16)),
        in_specs=[smem, vmem, vmem, vmem, hbm],
        out_specs=(vmem, vmem, hbm),
        scratch_shapes=[pltpu.VMEM((a.shape[2], items), f32), pltpu.VMEM(tail.shape, bf16), pltpu.SemaphoreType.DMA],
        input_output_aliases={4: 2},
        compiler_params=pltpu.CompilerParams(vmem_limit_bytes=24 << 20),
        cost_estimate=pl.CostEstimate(flops=1 << 34, bytes_accessed=1 << 24, transcendentals=0),
        name="own_items",
    )(core, a, sent, kept, tail)
    return users, item_sums


def other_items(core_ref, a_ref, got_ref, user_ref, item_ref, keep_ref, send_ref, total, users, items):
    core = core_ref[0]
    blocks, half, comps = a_ref.shape
    b = sent_factors(got_ref, blocks, comps)

    def counts_of(i):
        return got_ref[i * STEP : (i + 1) * STEP]

    def add_users(at, terms):
        users[at] = user_ref[at] + terms

    add_terms(a_ref, counts_of, b, add_users, total)
    rows = b.shape[0] // blocks
    items[...] = item_ref[...]
    place_items(b, total[...], items, 1 - core, rows)

    @pl.when(core == 0)
    def _():
        keep_ref[...] = users[...]
        send_ref[...] = items[...].astype(bf16)

    @pl.when(core != 0)
    def _():
        keep_ref[...] = items[...]
        send_ref[...] = users[...].astype(bf16)


def first_terms(core_ref, keep_ref, got_ref, out_ref):
    other = jnp.where(core_ref[0] == 0, 0.0, got_ref[...].astype(f32))
    out_ref[...] = (keep_ref[...] + other).astype(bf16)


def second_terms(core_ref, parts_ref, got_ref, new_ref, out_ref):
    total = jnp.sum(parts_ref[...].astype(f32), 0)
    new_ref[...] = prior_shape + total

    @pl.when(core_ref[0] == 0)
    def _():
        out_ref[...] = got_ref[...]

    @pl.when(core_ref[0] != 0)
    def _():
        out_ref[...] = jnp.broadcast_to(total.astype(bf16)[None], out_ref.shape)


def last_terms(core_ref, parts_ref, out_ref):
    blocks, rows, _ = out_ref.shape

    @pl.when(core_ref[0] == 0)
    def _():
        new = prior_shape + jnp.sum(parts_ref[...].astype(f32), 0)
        rounded = new.astype(bf16)
        rest = (new - rounded.astype(f32)).astype(bf16)
        out_ref[...] = jnp.zeros_like(out_ref)
        for i in range(new.shape[0] // rows):
            part = slice(i * rows, (i + 1) * rows)
            out_ref[2 * i] = rounded[part]
            out_ref[2 * i + 1] = rest[part]

    @pl.when(core_ref[0] != 0)
    def _():
        out_ref[...] = parts_ref[:, :rows, :]


def finish(core_ref, new_ref, parts_ref, got_ref, user_ref, item_ref):
    blocks, rows, comps = got_ref.shape

    @pl.when(core_ref[0] == 0)
    def _():
        user_ref[...] = new_ref[...]
        item_ref[...] = prior_shape + got_ref[...].astype(f32).reshape(blocks * rows, comps)

    @pl.when(core_ref[0] != 0)
    def _():
        for i in range(user_ref.shape[0] // rows):
            user_ref[i * rows : (i + 1) * rows] = got_ref[2 * i].astype(f32) + got_ref[2 * i + 1].astype(f32)
        item_ref[...] = prior_shape + parts_ref[:, rows:, :].astype(f32).reshape(blocks * rows, comps)


def small(kernel, out_shape, *operands, core=None, scratch=(), limit=24):
    vmem = pl.BlockSpec(memory_space=pltpu.VMEM)
    lead = () if core is None else (core,)
    return pl.pallas_call(
        kernel,
        out_shape=out_shape,
        in_specs=[pl.BlockSpec(memory_space=pltpu.SMEM)] * len(lead) + [vmem] * len(operands),
        out_specs=jax.tree.map(lambda _: vmem, out_shape),
        scratch_shapes=list(scratch),
        compiler_params=pltpu.CompilerParams(vmem_limit_bytes=limit << 20),
        name=kernel.__name__,
    )(*lead, *operands)


def body(n_group, n_shard, user_shape, user_rate, item_shape, item_rate, tile_rows, tile_cols, clicks, tile_count):
    own, comps = user_shape.shape
    items = item_shape.shape[0]
    edge = clicks.shape[1]
    chips = n_shard // 2
    both = ("group", "shard")
    swap = [(s, s ^ 1) for s in range(n_shard)]
    same_core = [[2 * r + c for r in range(chips)] for c in range(2)]
    users_or_items = [[g * n_shard + 2 * r for r in range(chips)] for g in range(n_group)]
    users_or_items += [[g * n_shard + 2 * r + 1 for g in range(n_group)] for r in range(chips)]
    core = (lax.axis_index("shard") & 1).astype(jnp.int32).reshape(1)

    copies = small(user_copies, jax.ShapeDtypeStruct((chips, own, comps), bf16), user_shape, user_rate, limit=56)
    a_mine = lax.all_to_all(copies, "shard", 0, 0, axis_index_groups=same_core)
    kept, tail, sent = pair_clicks(core, tile_rows, tile_cols, tile_count, clicks, item_shape, item_rate, chips)
    other = lax.ppermute(sent, "shard", swap)
    whole = (chips, own, comps)
    total = pltpu.VMEM((comps, items), f32)
    users, item_sums = near_items(core, a_mine, sent, kept, tail)
    keep, send = small(
        other_items, (pltpu.VMEM(whole, f32), pltpu.VMEM(whole, bf16)), a_mine, other, users, item_sums,
        core=core, scratch=(total, pltpu.VMEM(whole, f32), pltpu.VMEM(whole, f32)),
    )
    got = lax.ppermute(send, "shard", swap)
    terms = small(first_terms, jax.ShapeDtypeStruct(whole, bf16), keep, got, core=core)
    parts = lax.all_to_all(terms, both, 0, 0, axis_index_groups=users_or_items)
    new, terms = small(
        second_terms, (jax.ShapeDtypeStruct((own, comps), f32), jax.ShapeDtypeStruct(whole, bf16)), parts, got, core=core
    )
    parts = lax.all_to_all(terms, both, 0, 0, axis_index_groups=users_or_items)
    last = small(last_terms, jax.ShapeDtypeStruct((n_group, items // n_group, comps), bf16), parts, core=core)
    got = lax.ppermute(last, "shard", swap)
    return small(
        finish, (jax.ShapeDtypeStruct((own, comps), f32), jax.ShapeDtypeStruct((items, comps), f32)), new, parts, got, core=core
    )


def solution(mesh):
    return jax.shard_map(
        functools.partial(body, mesh.shape["group"], mesh.shape["shard"]),
        mesh=mesh,
        in_specs=(
            P(("group", "shard"), None),
            P(("group", "shard"), None),
            P("shard", None),
            P("shard", None),
            P(("group", "shard")),
            P(("group", "shard")),
            P(("group", "shard"), None, None),
            P(("group", "shard")),
        ),
        out_specs=(P(("group", "shard"), None), P("shard", None)),
        check_vma=False,
    )
```

```python
import functools
import jax
import jax.numpy as jnp
from jax import lax
from jax.experimental import pallas as pl
from jax.experimental.pallas import tpu as pltpu
from jax.sharding import PartitionSpec as P

CHUNK = 16
STEP = 4

prior_shape = 0.3
f32 = jnp.float32
bf16 = jnp.bfloat16
ROWS = (((0,), (0,)), ((), ()))
LANES = (((1,), (1,)), ((), ()))


def factors(shape, rate):
    y = shape + 6.0
    u = shape * (shape + 5.0)
    below = (2.0 * shape + 5.0) * ((3.0 * u + 20.0) * u + 24.0) / (u * ((u + 10.0) * u + 24.0))
    w = 1.0 / y
    v = w * w
    tail = 0.5 * w + v * (1.0 / 12.0 - v * (1.0 / 120.0 - v * (1.0 / 252.0)))
    return (y / rate * jnp.exp(-(tail + below))).astype(bf16)


def user_copies(shape_ref, rate_ref, out_ref):
    out_ref[...] = jnp.broadcast_to(factors(shape_ref[...], rate_ref[...])[None], out_ref.shape)


def add_clicks(slots, edge, core_ref, rows_ref, cols_ref, count_ref, clicks_ref, shape_ref, rate_ref, kept_ref, tail_ref, sent_ref, total, held, staged, sems):
    chunks = slots // CHUNK
    count = count_ref[0]
    blocks, _, items = total.shape
    half = staged.shape[1]
    near = kept_ref.shape[0]

    def copy(c):
        part = pl.ds(c * CHUNK, CHUNK)
        return pltpu.make_async_copy(clicks_ref.at[part], held.at[part], sems.at[c])

    for c in range(chunks):
        @pl.when(c * CHUNK < count)
        def _():
            copy(c).start()

    def clear(r, carry):
        total[r] = jnp.zeros(total.shape[1:], f32)
        return carry

    lax.fori_loop(0, blocks, clear, 0)
    wide = items // edge
    for j in range(items // half):
        part = slice(j * half, (j + 1) * half)
        lanes = slice(j % wide * edge, (j % wide + 1) * edge)
        sent_ref[blocks + j // wide, :, lanes] = factors(shape_ref[part], rate_ref[part])

    def add(t, carry):
        row = rows_ref[t]
        cols = pl.ds(pl.multiple_of(cols_ref[t] * edge, edge), edge)
        total[row, :, cols] += held[t].astype(f32)
        return carry

    for c in range(chunks):
        @pl.when(c * CHUNK < count)
        def _():
            copy(c).wait()
            lax.fori_loop(c * CHUNK, jnp.minimum(count, (c + 1) * CHUNK), add, 0)

    first = core_ref[0] * half
    kept = pl.ds(pl.multiple_of(first, half), half)
    sent = pl.ds(pl.multiple_of(half - first, half), half)

    def keep_tail(r, carry):
        staged[r] = total[near + r, kept, :].astype(bf16)
        return carry

    def keep(r, carry):
        kept_ref[r] = total[r, kept, :].astype(bf16)
        return carry

    def send(r, carry):
        sent_ref[r] = total[r, sent, :].astype(bf16)
        return carry

    lax.fori_loop(0, blocks - near, keep_tail, 0)
    out = pltpu.make_async_copy(staged, tail_ref, sems.at[chunks])
    out.start()
    lax.fori_loop(0, near, keep, 0)
    lax.fori_loop(0, blocks, send, 0)
    out.wait()


def pair_clicks(core, tile_rows, tile_cols, tile_count, clicks, item_shape, item_rate, blocks):
    slots, edge, _ = clicks.shape
    items, comps = item_shape.shape
    half = edge // 2
    smem, vmem = pl.BlockSpec(memory_space=pltpu.SMEM), pl.BlockSpec(memory_space=pltpu.VMEM)
    return pl.pallas_call(
        functools.partial(add_clicks, slots, edge),
        out_shape=(
            pltpu.VMEM((blocks - STEP, half, items), bf16),
            pltpu.HBM((STEP, half, items), bf16),
            pltpu.VMEM((blocks + comps // half, half, items), bf16),
        ),
        in_specs=[smem] * 4 + [pl.BlockSpec(memory_space=pltpu.HBM), vmem, vmem],
        out_specs=(vmem, pl.BlockSpec(memory_space=pltpu.HBM), vmem),
        scratch_shapes=[
            pltpu.VMEM((blocks, edge, items), f32),
            pltpu.VMEM((slots, edge, edge), bf16),
            pltpu.VMEM((STEP, half, items), bf16),
            pltpu.SemaphoreType.DMA((slots // CHUNK + 1,)),
        ],
        compiler_params=pltpu.CompilerParams(vmem_limit_bytes=56 << 20),
        cost_estimate=pl.CostEstimate(flops=slots * edge * edge, bytes_accessed=2 * slots * edge * edge, transcendentals=0),
        name="pair_clicks",
    )(core, tile_rows, tile_cols, tile_count, clicks, item_shape, item_rate)


def sent_factors(sent_ref, blocks, comps):
    return jnp.concatenate(
        [sent_ref[q, :, j : j + comps] for q in range(blocks, sent_ref.shape[0]) for j in range(0, sent_ref.shape[2], comps)],
        0,
    )


def add_terms(a_ref, counts_of, b, add_users, total):
    blocks, half, comps = a_ref.shape
    rows = STEP * half
    total[...] = jnp.zeros_like(total)
    for i in range(blocks // STEP):
        at = pl.ds(i * STEP, STEP)
        a = a_ref[at].reshape(rows, comps)
        denom = lax.dot_general(a, b, LANES, preferred_element_type=f32)
        ratio = (counts_of(i).reshape(rows, -1).astype(f32) / denom).astype(bf16)
        product = jnp.dot(ratio, b, preferred_element_type=f32)
        add_users(at, (a.astype(f32) * product).reshape(STEP, half, comps))
        total[...] += lax.dot_general(a, ratio, ROWS, preferred_element_type=f32)


def place_items(b, sums, out_ref, part, items_of):
    blocks = out_ref.shape[0]
    terms = (b.astype(f32) * sums.T).reshape(blocks, items_of, -1)
    out_ref[:, pl.ds(pl.multiple_of(part * items_of, items_of), items_of), :] = terms


def own_items(core_ref, a_ref, sent_ref, kept_ref, tail_ref, user_ref, item_ref, same_ref, total, held, sem):
    blocks, _, comps = a_ref.shape
    copy = pltpu.make_async_copy(tail_ref, held, sem)
    copy.start()
    b = sent_factors(sent_ref, blocks, comps)

    def counts_of(i):
        if (i + 1) * STEP == kept_ref.shape[0]:
            copy.wait()
        if (i + 1) * STEP <= kept_ref.shape[0]:
            return kept_ref[i * STEP : (i + 1) * STEP]
        return held[...]

    def add_users(at, terms):
        user_ref[at] = terms

    add_terms(a_ref, counts_of, b, add_users, total)
    place_items(b, total[...], item_ref, core_ref[0], b.shape[0] // blocks)


def near_items(core, a, sent, kept, tail):
    smem, vmem, hbm = (pl.BlockSpec(memory_space=m) for m in (pltpu.SMEM, pltpu.VMEM, pltpu.HBM))
    items = sent.shape[2]
    users, item_sums, _ = pl.pallas_call(
        own_items,
        out_shape=(pltpu.VMEM(a.shape, f32), pltpu.VMEM(a.shape, f32), pltpu.HBM(tail.shape, bf16)),
        in_specs=[smem, vmem, vmem, vmem, hbm],
        out_specs=(vmem, vmem, hbm),
        scratch_shapes=[pltpu.VMEM((a.shape[2], items), f32), pltpu.VMEM(tail.shape, bf16), pltpu.SemaphoreType.DMA],
        input_output_aliases={4: 2},
        compiler_params=pltpu.CompilerParams(vmem_limit_bytes=24 << 20),
        cost_estimate=pl.CostEstimate(flops=1 << 34, bytes_accessed=1 << 24, transcendentals=0),
        name="own_items",
    )(core, a, sent, kept, tail)
    return users, item_sums


def other_items(core_ref, a_ref, got_ref, user_ref, item_ref, keep_ref, send_ref, total, users, items):
    core = core_ref[0]
    blocks, half, comps = a_ref.shape
    b = sent_factors(got_ref, blocks, comps)

    def counts_of(i):
        return got_ref[i * STEP : (i + 1) * STEP]

    def add_users(at, terms):
        users[at] = user_ref[at] + terms

    add_terms(a_ref, counts_of, b, add_users, total)
    rows = b.shape[0] // blocks
    items[...] = item_ref[...]
    place_items(b, total[...], items, 1 - core, rows)

    @pl.when(core == 0)
    def _():
        keep_ref[...] = users[...]
        send_ref[...] = items[...].astype(bf16)

    @pl.when(core != 0)
    def _():
        keep_ref[...] = items[...]
        send_ref[...] = users[...].astype(bf16)


def first_terms(core_ref, keep_ref, sent_ref, out_ref):
    other = jnp.where(core_ref[0] == 0, 0.0, sent_ref[0].astype(f32))
    out_ref[...] = (keep_ref[...] + other).astype(bf16)


def second_terms(core_ref, parts_ref, sent_ref, new_ref, out_ref):
    total = jnp.sum(parts_ref[...].astype(f32), 0)
    new_ref[...] = prior_shape + total

    @pl.when(core_ref[0] == 0)
    def _():
        out_ref[...] = sent_ref[1]

    @pl.when(core_ref[0] != 0)
    def _():
        out_ref[...] = jnp.broadcast_to(total.astype(bf16)[None], out_ref.shape)


def finish(core_ref, new_ref, parts_ref, user_ref, item_ref):
    rows = parts_ref.shape[2] // 2

    @pl.when(core_ref[0] == 0)
    def _():
        user_ref[...] = new_ref[...]
        item_ref[...] = prior_shape + parts_ref[1, :, :rows].astype(f32).reshape(item_ref.shape)

    @pl.when(core_ref[0] != 0)
    def _():
        user_ref[...] = prior_shape + jnp.sum(parts_ref[0].astype(f32), 0)
        item_ref[...] = prior_shape + parts_ref[1, :, rows:].astype(f32).reshape(item_ref.shape)


def small(kernel, out_shape, *operands, core=None, scratch=(), limit=24):
    vmem = pl.BlockSpec(memory_space=pltpu.VMEM)
    lead = () if core is None else (core,)
    return pl.pallas_call(
        kernel,
        out_shape=out_shape,
        in_specs=[pl.BlockSpec(memory_space=pltpu.SMEM)] * len(lead) + [vmem] * len(operands),
        out_specs=jax.tree.map(lambda _: vmem, out_shape),
        scratch_shapes=list(scratch),
        compiler_params=pltpu.CompilerParams(vmem_limit_bytes=limit << 20),
        name=kernel.__name__,
    )(*lead, *operands)


def body(n_group, n_shard, user_shape, user_rate, item_shape, item_rate, tile_rows, tile_cols, clicks, tile_count):
    own, comps = user_shape.shape
    items = item_shape.shape[0]
    edge = clicks.shape[1]
    chips = n_shard // 2
    both = ("group", "shard")
    swap = [(s, s ^ 1) for s in range(n_shard)]
    pairs = [[2 * r, 2 * r + 1] for r in range(chips)]
    same_core = [[2 * r + c for r in range(chips)] for c in range(2)]
    users_or_items = [[g * n_shard + 2 * r for r in range(chips)] for g in range(n_group)]
    users_or_items += [[g * n_shard + 2 * r + 1 for g in range(n_group)] for r in range(chips)]
    core = (lax.axis_index("shard") & 1).astype(jnp.int32).reshape(1)

    copies = small(user_copies, jax.ShapeDtypeStruct((chips, own, comps), bf16), user_shape, user_rate, limit=56)
    a_mine = lax.all_to_all(copies, "shard", 0, 0, axis_index_groups=same_core)
    kept, tail, sent = pair_clicks(core, tile_rows, tile_cols, tile_count, clicks, item_shape, item_rate, chips)
    other = lax.ppermute(sent, "shard", swap)
    whole = (chips, own, comps)
    users, item_sums = near_items(core, a_mine, sent, kept, tail)
    keep, send = small(
        other_items, (pltpu.VMEM(whole, f32), pltpu.VMEM(whole, bf16)), a_mine, other, users, item_sums,
        core=core, scratch=(pltpu.VMEM((comps, items), f32), pltpu.VMEM(whole, f32), pltpu.VMEM(whole, f32)),
    )
    sent = lax.all_gather(send, "shard", axis_index_groups=pairs)
    terms = small(first_terms, jax.ShapeDtypeStruct(whole, bf16), keep, sent, core=core)
    parts = lax.all_to_all(terms, both, 0, 0, axis_index_groups=users_or_items)
    new, terms = small(
        second_terms, (jax.ShapeDtypeStruct((own, comps), f32), jax.ShapeDtypeStruct(whole, bf16)), parts, sent, core=core
    )
    parts = lax.all_to_all(terms, both, 0, 0, axis_index_groups=users_or_items)
    parts = lax.all_gather(parts, "shard", axis_index_groups=pairs)
    return small(
        finish, (jax.ShapeDtypeStruct((own, comps), f32), jax.ShapeDtypeStruct((items, comps), f32)), new, parts, core=core
    )


def solution(mesh):
    return jax.shard_map(
        functools.partial(body, mesh.shape["group"], mesh.shape["shard"]),
        mesh=mesh,
        in_specs=(
            P(("group", "shard"), None),
            P(("group", "shard"), None),
            P("shard", None),
            P("shard", None),
            P(("group", "shard")),
            P(("group", "shard")),
            P(("group", "shard"), None, None),
            P(("group", "shard")),
        ),
        out_specs=(P(("group", "shard"), None), P("shard", None)),
        check_vma=False,
    )
```

```python
import functools
import jax
import jax.numpy as jnp
from jax import lax
from jax.experimental import pallas as pl
from jax.experimental.pallas import tpu as pltpu
from jax.sharding import PartitionSpec as P

CHUNK = 16
STEP = 4
UNROLL = 4
FAR = 2

prior_shape = 0.3
f32 = jnp.float32
bf16 = jnp.bfloat16
ROWS = (((0,), (0,)), ((), ()))
LANES = (((1,), (1,)), ((), ()))


def factors(shape, rate):
    y = shape + 6.0
    u = shape * (shape + 5.0)
    below = (2.0 * shape + 5.0) * ((3.0 * u + 20.0) * u + 24.0) / (u * ((u + 10.0) * u + 24.0))
    w = 1.0 / y
    v = w * w
    tail = 0.5 * w + v * (1.0 / 12.0 - v * (1.0 / 120.0 - v * (1.0 / 252.0)))
    return (y / rate * jnp.exp(-(tail + below))).astype(bf16)


def this_core():
    return lax.axis_index("shard") & 1


def user_copies(shape_ref, rate_ref, out_ref):
    out_ref[...] = jnp.broadcast_to(factors(shape_ref[...], rate_ref[...])[None], out_ref.shape)


def add_clicks(
    slots, edge, rows_in, cols_in, count_in, clicks_ref, shape_in, rate_in, kept_ref, tail_ref, sent_ref,
    total, held, staged, rows_ref, cols_ref, count_ref, shape_ref, rate_ref, sems, more_sems,
):
    chunks = slots // CHUNK
    blocks, items = total.shape[0] - 1, total.shape[2]
    half = staged.shape[1]
    near = kept_ref.shape[0]

    def copy(c):
        part = pl.ds(c * CHUNK, CHUNK)
        return pltpu.make_async_copy(clicks_ref.at[part], held.at[part], sems.at[c])

    pairs = ((shape_in, shape_ref), (rate_in, rate_ref), (rows_in, rows_ref), (cols_in, cols_ref), (count_in, count_ref))
    more = [pltpu.make_async_copy(source, target, more_sems.at[i]) for i, (source, target) in enumerate(pairs)]
    for one in more:
        one.start()
    for c in range(chunks):
        copy(c).start()

    def clear(r, carry):
        total[r] = jnp.zeros(total.shape[1:], f32)
        return carry

    lax.fori_loop(0, blocks, clear, 0)
    for one in more[2:]:
        one.wait()
    count = count_ref[0]

    def add(i, carry):
        slots_of = [i * UNROLL + k for k in range(UNROLL)]
        rows = [jnp.where(t < count, rows_ref[t], blocks) for t in slots_of]
        cols = [pl.ds(pl.multiple_of(cols_ref[t] * edge, edge), edge) for t in slots_of]
        for t, row, part in zip(slots_of, rows, cols):
            total[row, :, part] += held[t].astype(f32)
        return carry

    for c in range(chunks):
        copy(c).wait()
        steps = jnp.clip(count - c * CHUNK, 0, CHUNK)
        lax.fori_loop(c * CHUNK // UNROLL, (c * CHUNK + steps + UNROLL - 1) // UNROLL, add, 0)

    first = this_core() * half
    kept = pl.ds(pl.multiple_of(first, half), half)
    sent = pl.ds(pl.multiple_of(half - first, half), half)

    def keep_tail(r, carry):
        staged[r] = total[near + r, kept, :].astype(bf16)
        return carry

    lax.fori_loop(0, blocks - near, keep_tail, 0)
    out = pltpu.make_async_copy(staged, tail_ref, sems.at[chunks])
    out.start()
    more[0].wait()
    more[1].wait()
    wide = items // edge
    parts = items // half
    each = blocks // parts
    for j in range(parts):
        part = slice(j * half, (j + 1) * half)
        lanes = slice(j % wide * edge, (j % wide + 1) * edge)
        sent_ref[blocks + j // wide, :, lanes] = factors(shape_ref[part], rate_ref[part])
        for r in range(j * each, (j + 1) * each):
            sent_ref[r] = total[r, sent, :].astype(bf16)
            if r < near:
                kept_ref[r] = total[r, kept, :].astype(bf16)
    out.wait()


def pair_clicks(tile_rows, tile_cols, tile_count, clicks, item_shape, item_rate, blocks):
    slots, edge, _ = clicks.shape
    items, comps = item_shape.shape
    half = edge // 2
    vmem, hbm = pl.BlockSpec(memory_space=pltpu.VMEM), pl.BlockSpec(memory_space=pltpu.HBM)
    return pl.pallas_call(
        functools.partial(add_clicks, slots, edge),
        out_shape=(
            pltpu.VMEM((blocks - FAR, half, items), bf16),
            pltpu.HBM((FAR, half, items), bf16),
            pltpu.VMEM((blocks + comps // half, half, items), bf16),
        ),
        in_specs=[hbm] * 6,
        out_specs=(vmem, hbm, vmem),
        scratch_shapes=[
            pltpu.VMEM((blocks + 1, edge, items), f32),
            pltpu.VMEM((slots, edge, edge), bf16),
            pltpu.VMEM((FAR, half, items), bf16),
            pltpu.SMEM(tile_rows.shape, jnp.int32),
            pltpu.SMEM(tile_cols.shape, jnp.int32),
            pltpu.SMEM(tile_count.shape, jnp.int32),
            pltpu.VMEM(item_shape.shape, f32),
            pltpu.VMEM(item_rate.shape, f32),
            pltpu.SemaphoreType.DMA((slots // CHUNK + 1,)),
            pltpu.SemaphoreType.DMA((5,)),
        ],
        compiler_params=pltpu.CompilerParams(vmem_limit_bytes=56 << 20),
        cost_estimate=pl.CostEstimate(flops=slots * edge * edge, bytes_accessed=2 * slots * edge * edge, transcendentals=0),
        name="pair_clicks",
    )(tile_rows, tile_cols, tile_count, clicks, item_shape, item_rate)


def sent_factors(sent_ref, blocks, comps):
    return jnp.concatenate(
        [sent_ref[q, :, j : j + comps] for q in range(blocks, sent_ref.shape[0]) for j in range(0, sent_ref.shape[2], comps)],
        0,
    )


def add_terms(a_ref, counts_of, b, add_users, total):
    blocks, half, comps = a_ref.shape
    rows = STEP * half
    total[...] = jnp.zeros_like(total)
    for i in range(blocks // STEP):
        at = pl.ds(i * STEP, STEP)
        a = a_ref[at].reshape(rows, comps)
        denom = lax.dot_general(a, b, LANES, preferred_element_type=f32)
        ratio = (counts_of(i).reshape(rows, -1).astype(f32) / denom).astype(bf16)
        product = jnp.dot(ratio, b, preferred_element_type=f32)
        add_users(at, (a.astype(f32) * product).reshape(STEP, half, comps))
        total[...] += lax.dot_general(a, ratio, ROWS, preferred_element_type=f32)


def place_items(b, sums, out_ref, part, items_of):
    blocks = out_ref.shape[0]
    terms = (b.astype(f32) * sums.T).reshape(blocks, items_of, -1)
    out_ref[:, pl.ds(pl.multiple_of(part * items_of, items_of), items_of), :] = terms


def own_items(a_ref, sent_ref, kept_ref, tail_ref, user_ref, item_ref, same_ref, total, held, sem):
    blocks, _, comps = a_ref.shape
    copy = pltpu.make_async_copy(tail_ref, held, sem)
    copy.start()
    b = sent_factors(sent_ref, blocks, comps)

    def counts_of(i):
        if i == blocks // STEP - 2:
            copy.wait()
        if (i + 1) * STEP <= kept_ref.shape[0]:
            return kept_ref[i * STEP : (i + 1) * STEP]
        return jnp.concatenate([kept_ref[i * STEP :], held[...]], 0)

    def add_users(at, terms):
        user_ref[at] = terms

    add_terms(a_ref, counts_of, b, add_users, total)
    place_items(b, total[...], item_ref, this_core(), b.shape[0] // blocks)


def near_items(a, sent, kept, tail):
    vmem, hbm = pl.BlockSpec(memory_space=pltpu.VMEM), pl.BlockSpec(memory_space=pltpu.HBM)
    items = sent.shape[2]
    users, item_sums, _ = pl.pallas_call(
        own_items,
        out_shape=(pltpu.VMEM(a.shape, f32), pltpu.VMEM(a.shape, f32), pltpu.HBM(tail.shape, bf16)),
        in_specs=[vmem, vmem, vmem, hbm],
        out_specs=(vmem, vmem, hbm),
        scratch_shapes=[pltpu.VMEM((a.shape[2], items), f32), pltpu.VMEM(tail.shape, bf16), pltpu.SemaphoreType.DMA],
        input_output_aliases={3: 2},
        compiler_params=pltpu.CompilerParams(vmem_limit_bytes=24 << 20),
        cost_estimate=pl.CostEstimate(flops=1 << 34, bytes_accessed=1 << 24, transcendentals=0),
        name="own_items",
    )(a, sent, kept, tail)
    return users, item_sums


def other_items(a_ref, got_ref, user_ref, item_ref, keep_ref, send_ref, total, users, items):
    core = this_core()
    blocks, half, comps = a_ref.shape
    b = sent_factors(got_ref, blocks, comps)

    def counts_of(i):
        return got_ref[i * STEP : (i + 1) * STEP]

    def add_users(at, terms):
        users[at] = user_ref[at] + terms

    add_terms(a_ref, counts_of, b, add_users, total)
    rows = b.shape[0] // blocks
    items[...] = item_ref[...]
    place_items(b, total[...], items, 1 - core, rows)

    @pl.when(core == 0)
    def _():
        keep_ref[...] = users[...]
        send_ref[...] = items[...].astype(bf16)

    @pl.when(core != 0)
    def _():
        keep_ref[...] = items[...]
        send_ref[...] = users[...].astype(bf16)


def first_terms(keep_ref, sent_ref, out_ref):
    other = jnp.where(this_core() == 0, 0.0, sent_ref[0].astype(f32))
    out_ref[...] = (keep_ref[...] + other).astype(bf16)


def second_terms(parts_ref, sent_ref, new_ref, out_ref):
    total = jnp.sum(parts_ref[...].astype(f32), 0)
    new_ref[...] = prior_shape + total

    @pl.when(this_core() == 0)
    def _():
        out_ref[...] = sent_ref[1]

    @pl.when(this_core() != 0)
    def _():
        out_ref[...] = jnp.broadcast_to(total.astype(bf16)[None], out_ref.shape)


def finish(new_ref, parts_ref, user_ref, item_ref):
    rows = parts_ref.shape[2] // 2

    @pl.when(this_core() == 0)
    def _():
        user_ref[...] = new_ref[...]
        item_ref[...] = prior_shape + parts_ref[1, :, :rows].astype(f32).reshape(item_ref.shape)

    @pl.when(this_core() != 0)
    def _():
        user_ref[...] = prior_shape + jnp.sum(parts_ref[0].astype(f32), 0)
        item_ref[...] = prior_shape + parts_ref[1, :, rows:].astype(f32).reshape(item_ref.shape)


def small(kernel, out_shape, *operands, scratch=(), limit=24):
    vmem = pl.BlockSpec(memory_space=pltpu.VMEM)
    return pl.pallas_call(
        kernel,
        out_shape=out_shape,
        in_specs=[vmem] * len(operands),
        out_specs=jax.tree.map(lambda _: vmem, out_shape),
        scratch_shapes=list(scratch),
        compiler_params=pltpu.CompilerParams(vmem_limit_bytes=limit << 20),
        name=kernel.__name__,
    )(*operands)


def body(n_group, n_shard, user_shape, user_rate, item_shape, item_rate, tile_rows, tile_cols, clicks, tile_count):
    own, comps = user_shape.shape
    items = item_shape.shape[0]
    edge = clicks.shape[1]
    chips = n_shard // 2
    both = ("group", "shard")
    swap = [(s, s ^ 1) for s in range(n_shard)]
    pairs = [[2 * r, 2 * r + 1] for r in range(chips)]
    same_core = [[2 * r + c for r in range(chips)] for c in range(2)]
    users_or_items = [[g * n_shard + 2 * r for r in range(chips)] for g in range(n_group)]
    users_or_items += [[g * n_shard + 2 * r + 1 for g in range(n_group)] for r in range(chips)]

    copies = small(user_copies, jax.ShapeDtypeStruct((chips, own, comps), bf16), user_shape, user_rate, limit=56)
    a_mine = lax.all_to_all(copies, "shard", 0, 0, axis_index_groups=same_core)
    kept, tail, sent = pair_clicks(tile_rows, tile_cols, tile_count, clicks, item_shape, item_rate, chips)
    other = lax.ppermute(sent, "shard", swap)
    whole = (chips, own, comps)
    users, item_sums = near_items(a_mine, sent, kept, tail)
    keep, send = small(
        other_items, (pltpu.VMEM(whole, f32), pltpu.VMEM(whole, bf16)), a_mine, other, users, item_sums,
        scratch=(pltpu.VMEM((comps, items), f32), pltpu.VMEM(whole, f32), pltpu.VMEM(whole, f32)),
    )
    sent = lax.all_gather(send, "shard", axis_index_groups=pairs)
    terms = small(first_terms, jax.ShapeDtypeStruct(whole, bf16), keep, sent)
    parts = lax.all_to_all(terms, both, 0, 0, axis_index_groups=users_or_items)
    new, terms = small(
        second_terms, (jax.ShapeDtypeStruct((own, comps), f32), jax.ShapeDtypeStruct(whole, bf16)), parts, sent
    )
    parts = lax.all_to_all(terms, both, 0, 0, axis_index_groups=users_or_items)
    parts = lax.all_gather(parts, "shard", axis_index_groups=pairs)
    return small(
        finish, (jax.ShapeDtypeStruct((own, comps), f32), jax.ShapeDtypeStruct((items, comps), f32)), new, parts
    )


def solution(mesh):
    return jax.shard_map(
        functools.partial(body, mesh.shape["group"], mesh.shape["shard"]),
        mesh=mesh,
        in_specs=(
            P(("group", "shard"), None),
            P(("group", "shard"), None),
            P("shard", None),
            P("shard", None),
            P(("group", "shard")),
            P(("group", "shard")),
            P(("group", "shard"), None, None),
            P(("group", "shard")),
        ),
        out_specs=(P(("group", "shard"), None), P("shard", None)),
        check_vma=False,
    )
```

```python
import functools
import jax
import jax.numpy as jnp
from jax import lax
from jax.experimental import pallas as pl
from jax.experimental.pallas import tpu as pltpu
from jax.sharding import PartitionSpec as P

CHUNK = 16
UNROLL = 4
FAR = 2

prior_shape = 0.3
f32 = jnp.float32
bf16 = jnp.bfloat16
ROWS = (((0,), (0,)), ((), ()))
LANES = (((1,), (1,)), ((), ()))


def factors(shape, rate):
    y = shape + 6.0
    u = shape * (shape + 5.0)
    below = (2.0 * shape + 5.0) * ((3.0 * u + 20.0) * u + 24.0) / (u * ((u + 10.0) * u + 24.0))
    w = 1.0 / y
    v = w * w
    tail = 0.5 * w + v * (1.0 / 12.0 - v * (1.0 / 120.0 - v * (1.0 / 252.0)))
    return (y / rate * jnp.exp(-(tail + below))).astype(bf16)


def this_core():
    return lax.axis_index("shard") & 1


def user_copies(shape_ref, rate_ref, out_ref):
    out_ref[...] = jnp.broadcast_to(factors(shape_ref[...], rate_ref[...])[None], out_ref.shape)


def add_clicks(
    slots, edge, rows_in, cols_in, count_in, clicks_ref, shape_in, rate_in, kept_ref, tail_ref, sent_ref,
    total, held, staged, rows_ref, cols_ref, count_ref, shape_ref, rate_ref, sems, more_sems,
):
    chunks = slots // CHUNK
    blocks, items = total.shape[0] - 1, total.shape[2]
    half = staged.shape[1]
    near = kept_ref.shape[0]

    def copy(c):
        part = pl.ds(c * CHUNK, CHUNK)
        return pltpu.make_async_copy(clicks_ref.at[part], held.at[part], sems.at[c])

    pairs = ((shape_in, shape_ref), (rate_in, rate_ref), (rows_in, rows_ref), (cols_in, cols_ref), (count_in, count_ref))
    more = [pltpu.make_async_copy(source, target, more_sems.at[i]) for i, (source, target) in enumerate(pairs)]
    for one in more:
        one.start()
    for c in range(chunks):
        copy(c).start()

    def clear(r, carry):
        total[r] = jnp.zeros(total.shape[1:], f32)
        return carry

    lax.fori_loop(0, blocks, clear, 0)
    for one in more[2:]:
        one.wait()
    count = count_ref[0]

    def add(i, carry):
        slots_of = [i * UNROLL + k for k in range(UNROLL)]
        rows = [jnp.where(t < count, rows_ref[t], blocks) for t in slots_of]
        cols = [pl.ds(pl.multiple_of(cols_ref[t] * edge, edge), edge) for t in slots_of]
        for t, row, part in zip(slots_of, rows, cols):
            total[row, :, part] += held[t].astype(f32)
        return carry

    for c in range(chunks):
        copy(c).wait()
        steps = jnp.clip(count - c * CHUNK, 0, CHUNK)
        lax.fori_loop(c * CHUNK // UNROLL, (c * CHUNK + steps + UNROLL - 1) // UNROLL, add, 0)

    first = this_core() * half
    kept = pl.ds(pl.multiple_of(first, half), half)
    sent = pl.ds(pl.multiple_of(half - first, half), half)

    def keep_tail(r, carry):
        staged[r] = total[near + r, kept, :].astype(bf16)
        return carry

    lax.fori_loop(0, blocks - near, keep_tail, 0)
    out = pltpu.make_async_copy(staged, tail_ref, sems.at[chunks])
    out.start()
    more[0].wait()
    more[1].wait()
    wide = items // edge
    parts = items // half
    each = blocks // parts
    for j in range(parts):
        part = slice(j * half, (j + 1) * half)
        lanes = slice(j % wide * edge, (j % wide + 1) * edge)
        sent_ref[blocks + j // wide, :, lanes] = factors(shape_ref[part], rate_ref[part])
        for r in range(j * each, (j + 1) * each):
            sent_ref[r] = total[r, sent, :].astype(bf16)
            if r < near:
                kept_ref[r] = total[r, kept, :].astype(bf16)
    out.wait()


def pair_clicks(tile_rows, tile_cols, tile_count, clicks, item_shape, item_rate, blocks):
    slots, edge, _ = clicks.shape
    items, comps = item_shape.shape
    half = edge // 2
    vmem, hbm = pl.BlockSpec(memory_space=pltpu.VMEM), pl.BlockSpec(memory_space=pltpu.HBM)
    return pl.pallas_call(
        functools.partial(add_clicks, slots, edge),
        out_shape=(
            pltpu.VMEM((blocks - FAR, half, items), bf16),
            pltpu.HBM((FAR, half, items), bf16),
            pltpu.VMEM((blocks + comps // half, half, items), bf16),
        ),
        in_specs=[hbm] * 6,
        out_specs=(vmem, hbm, vmem),
        scratch_shapes=[
            pltpu.VMEM((blocks + 1, edge, items), f32),
            pltpu.VMEM((slots, edge, edge), bf16),
            pltpu.VMEM((FAR, half, items), bf16),
            pltpu.SMEM(tile_rows.shape, jnp.int32),
            pltpu.SMEM(tile_cols.shape, jnp.int32),
            pltpu.SMEM(tile_count.shape, jnp.int32),
            pltpu.VMEM(item_shape.shape, f32),
            pltpu.VMEM(item_rate.shape, f32),
            pltpu.SemaphoreType.DMA((slots // CHUNK + 1,)),
            pltpu.SemaphoreType.DMA((5,)),
        ],
        compiler_params=pltpu.CompilerParams(vmem_limit_bytes=56 << 20),
        cost_estimate=pl.CostEstimate(flops=slots * edge * edge, bytes_accessed=2 * slots * edge * edge, transcendentals=0),
        name="pair_clicks",
    )(tile_rows, tile_cols, tile_count, clicks, item_shape, item_rate)


def sent_factors(sent_ref, blocks, comps):
    return jnp.concatenate(
        [sent_ref[q, :, j : j + comps] for q in range(blocks, sent_ref.shape[0]) for j in range(0, sent_ref.shape[2], comps)],
        0,
    )


def add_terms(a_ref, cuts, counts_of, b, add_users, total):
    _, half, comps = a_ref.shape
    total[...] = jnp.zeros_like(total)
    for first, last in zip(cuts, cuts[1:]):
        at = pl.ds(first, last - first)
        rows = (last - first) * half
        a = a_ref[at].reshape(rows, comps)
        denom = lax.dot_general(a, b, LANES, preferred_element_type=f32)
        ratio = (counts_of(first, last).reshape(rows, -1).astype(f32) / denom).astype(bf16)
        product = jnp.dot(ratio, b, preferred_element_type=f32)
        add_users(at, (a.astype(f32) * product).reshape(-1, half, comps))
        total[...] += lax.dot_general(a, ratio, ROWS, preferred_element_type=f32)


def place_items(b, sums, out_ref, part, items_of):
    blocks = out_ref.shape[0]
    terms = (b.astype(f32) * sums.T).reshape(blocks, items_of, -1)
    out_ref[:, pl.ds(pl.multiple_of(part * items_of, items_of), items_of), :] = terms


def own_items(a_ref, sent_ref, kept_ref, tail_ref, user_ref, item_ref, same_ref, total, held, sem):
    blocks, _, comps = a_ref.shape
    copy = pltpu.make_async_copy(tail_ref, held, sem)
    copy.start()
    b = sent_factors(sent_ref, blocks, comps)

    near = kept_ref.shape[0]

    def counts_of(first, last):
        if last <= near:
            return kept_ref[first:last]
        copy.wait()
        return held[...]

    def add_users(at, terms):
        user_ref[at] = terms

    add_terms(a_ref, (0, near // 2, near, blocks), counts_of, b, add_users, total)
    place_items(b, total[...], item_ref, this_core(), b.shape[0] // blocks)


def near_items(a, sent, kept, tail):
    vmem, hbm = pl.BlockSpec(memory_space=pltpu.VMEM), pl.BlockSpec(memory_space=pltpu.HBM)
    items = sent.shape[2]
    users, item_sums, _ = pl.pallas_call(
        own_items,
        out_shape=(pltpu.VMEM(a.shape, f32), pltpu.VMEM(a.shape, f32), pltpu.HBM(tail.shape, bf16)),
        in_specs=[vmem, vmem, vmem, hbm],
        out_specs=(vmem, vmem, hbm),
        scratch_shapes=[pltpu.VMEM((a.shape[2], items), f32), pltpu.VMEM(tail.shape, bf16), pltpu.SemaphoreType.DMA],
        input_output_aliases={3: 2},
        compiler_params=pltpu.CompilerParams(vmem_limit_bytes=24 << 20),
        cost_estimate=pl.CostEstimate(flops=1 << 34, bytes_accessed=1 << 24, transcendentals=0),
        name="own_items",
    )(a, sent, kept, tail)
    return users, item_sums


def other_items(a_ref, got_ref, user_ref, item_ref, keep_ref, send_ref, total, users, items):
    core = this_core()
    blocks, half, comps = a_ref.shape
    b = sent_factors(got_ref, blocks, comps)

    def counts_of(first, last):
        return got_ref[first:last]

    def add_users(at, terms):
        users[at] = user_ref[at] + terms

    add_terms(a_ref, (0, blocks // 2, blocks), counts_of, b, add_users, total)
    rows = b.shape[0] // blocks
    items[...] = item_ref[...]
    place_items(b, total[...], items, 1 - core, rows)

    @pl.when(core == 0)
    def _():
        keep_ref[...] = users[...]
        send_ref[...] = items[...].astype(bf16)

    @pl.when(core != 0)
    def _():
        keep_ref[...] = items[...]
        send_ref[...] = users[...].astype(bf16)


def first_terms(keep_ref, sent_ref, out_ref):
    other = jnp.where(this_core() == 0, 0.0, sent_ref[0].astype(f32))
    out_ref[...] = (keep_ref[...] + other).astype(bf16)


def second_terms(parts_ref, sent_ref, new_ref, out_ref):
    total = jnp.sum(parts_ref[...].astype(f32), 0)
    new_ref[...] = prior_shape + total

    @pl.when(this_core() == 0)
    def _():
        out_ref[...] = sent_ref[1]

    @pl.when(this_core() != 0)
    def _():
        out_ref[...] = jnp.broadcast_to(total.astype(bf16)[None], out_ref.shape)


def finish(new_ref, parts_ref, user_ref, item_ref):
    rows = parts_ref.shape[2] // 2

    @pl.when(this_core() == 0)
    def _():
        user_ref[...] = new_ref[...]
        item_ref[...] = prior_shape + parts_ref[1, :, :rows].astype(f32).reshape(item_ref.shape)

    @pl.when(this_core() != 0)
    def _():
        user_ref[...] = prior_shape + jnp.sum(parts_ref[0].astype(f32), 0)
        item_ref[...] = prior_shape + parts_ref[1, :, rows:].astype(f32).reshape(item_ref.shape)


def small(kernel, out_shape, *operands, scratch=(), limit=24):
    vmem = pl.BlockSpec(memory_space=pltpu.VMEM)
    return pl.pallas_call(
        kernel,
        out_shape=out_shape,
        in_specs=[vmem] * len(operands),
        out_specs=jax.tree.map(lambda _: vmem, out_shape),
        scratch_shapes=list(scratch),
        compiler_params=pltpu.CompilerParams(vmem_limit_bytes=limit << 20),
        name=kernel.__name__,
    )(*operands)


def body(n_group, n_shard, user_shape, user_rate, item_shape, item_rate, tile_rows, tile_cols, clicks, tile_count):
    own, comps = user_shape.shape
    items = item_shape.shape[0]
    edge = clicks.shape[1]
    chips = n_shard // 2
    both = ("group", "shard")
    swap = [(s, s ^ 1) for s in range(n_shard)]
    pairs = [[2 * r, 2 * r + 1] for r in range(chips)]
    same_core = [[2 * r + c for r in range(chips)] for c in range(2)]
    users_or_items = [[g * n_shard + 2 * r for r in range(chips)] for g in range(n_group)]
    users_or_items += [[g * n_shard + 2 * r + 1 for g in range(n_group)] for r in range(chips)]

    copies = small(user_copies, jax.ShapeDtypeStruct((chips, own, comps), bf16), user_shape, user_rate, limit=56)
    a_mine = lax.all_to_all(copies, "shard", 0, 0, axis_index_groups=same_core)
    kept, tail, sent = pair_clicks(tile_rows, tile_cols, tile_count, clicks, item_shape, item_rate, chips)
    other = lax.ppermute(sent, "shard", swap)
    whole = (chips, own, comps)
    users, item_sums = near_items(a_mine, sent, kept, tail)
    keep, send = small(
        other_items, (pltpu.VMEM(whole, f32), pltpu.VMEM(whole, bf16)), a_mine, other, users, item_sums,
        scratch=(pltpu.VMEM((comps, items), f32), pltpu.VMEM(whole, f32), pltpu.VMEM(whole, f32)),
    )
    sent = lax.all_gather(send, "shard", axis_index_groups=pairs)
    terms = small(first_terms, jax.ShapeDtypeStruct(whole, bf16), keep, sent)
    parts = lax.all_to_all(terms, both, 0, 0, axis_index_groups=users_or_items)
    new, terms = small(
        second_terms, (jax.ShapeDtypeStruct((own, comps), f32), jax.ShapeDtypeStruct(whole, bf16)), parts, sent
    )
    parts = lax.all_to_all(terms, both, 0, 0, axis_index_groups=users_or_items)
    parts = lax.all_gather(parts, "shard", axis_index_groups=pairs)
    return small(
        finish, (jax.ShapeDtypeStruct((own, comps), f32), jax.ShapeDtypeStruct((items, comps), f32)), new, parts
    )


def solution(mesh):
    return jax.shard_map(
        functools.partial(body, mesh.shape["group"], mesh.shape["shard"]),
        mesh=mesh,
        in_specs=(
            P(("group", "shard"), None),
            P(("group", "shard"), None),
            P("shard", None),
            P("shard", None),
            P(("group", "shard")),
            P(("group", "shard")),
            P(("group", "shard"), None, None),
            P(("group", "shard")),
        ),
        out_specs=(P(("group", "shard"), None), P("shard", None)),
        check_vma=False,
    )
```

```python
import functools
import jax
import jax.numpy as jnp
from jax import lax
from jax.experimental import pallas as pl
from jax.experimental.pallas import tpu as pltpu
from jax.sharding import PartitionSpec as P

CHUNK = 16
UNROLL = 8
FAR = 2

prior_shape = 0.3
f32 = jnp.float32
bf16 = jnp.bfloat16
ROWS = (((0,), (0,)), ((), ()))
LANES = (((1,), (1,)), ((), ()))


def factors(shape, rate):
    y = shape + 6.0
    u = shape * (shape + 5.0)
    below = (2.0 * shape + 5.0) * ((3.0 * u + 20.0) * u + 24.0) / (u * ((u + 10.0) * u + 24.0))
    w = 1.0 / y
    v = w * w
    tail = 0.5 * w + v * (1.0 / 12.0 - v * (1.0 / 120.0 - v * (1.0 / 252.0)))
    return (y / rate * jnp.exp(-(tail + below))).astype(bf16)


def this_core():
    return lax.axis_index("shard") & 1


def user_copies(shape_ref, rate_ref, out_ref):
    out_ref[...] = jnp.broadcast_to(factors(shape_ref[...], rate_ref[...])[None], out_ref.shape)


def add_clicks(
    slots, edge, rows_in, cols_in, count_in, clicks_ref, shape_in, rate_in, kept_ref, tail_ref, sent_ref,
    total, held, staged, rows_ref, cols_ref, count_ref, shape_ref, rate_ref, sems, more_sems,
):
    chunks = slots // CHUNK
    blocks, items = total.shape[0] - 1, total.shape[2]
    half = staged.shape[1]
    near = kept_ref.shape[0]

    def copy(c):
        part = pl.ds(c * CHUNK, CHUNK)
        return pltpu.make_async_copy(clicks_ref.at[part], held.at[part], sems.at[c])

    pairs = ((shape_in, shape_ref), (rate_in, rate_ref), (rows_in, rows_ref), (cols_in, cols_ref), (count_in, count_ref))
    more = [pltpu.make_async_copy(source, target, more_sems.at[i]) for i, (source, target) in enumerate(pairs)]
    for one in more:
        one.start()
    for c in range(chunks):
        copy(c).start()

    def clear(r, carry):
        total[r] = jnp.zeros(total.shape[1:], f32)
        return carry

    lax.fori_loop(0, blocks, clear, 0)
    for one in more[2:]:
        one.wait()
    count = count_ref[0]

    def add(i, carry):
        slots_of = [i * UNROLL + k for k in range(UNROLL)]
        rows = [jnp.where(t < count, rows_ref[t], blocks) for t in slots_of]
        cols = [pl.ds(pl.multiple_of(cols_ref[t] * edge, edge), edge) for t in slots_of]
        for t, row, part in zip(slots_of, rows, cols):
            total[row, :, part] += held[t].astype(f32)
        return carry

    for c in range(chunks):
        copy(c).wait()
        steps = jnp.clip(count - c * CHUNK, 0, CHUNK)
        lax.fori_loop(c * CHUNK // UNROLL, (c * CHUNK + steps + UNROLL - 1) // UNROLL, add, 0)

    first = this_core() * half
    kept = pl.ds(pl.multiple_of(first, half), half)
    sent = pl.ds(pl.multiple_of(half - first, half), half)

    def keep_tail(r, carry):
        staged[r] = total[near + r, kept, :].astype(bf16)
        return carry

    lax.fori_loop(0, blocks - near, keep_tail, 0)
    out = pltpu.make_async_copy(staged, tail_ref, sems.at[chunks])
    out.start()
    more[0].wait()
    more[1].wait()
    wide = items // edge
    parts = items // half
    each = blocks // parts
    for j in range(parts):
        part = slice(j * half, (j + 1) * half)
        lanes = slice(j % wide * edge, (j % wide + 1) * edge)
        sent_ref[blocks + j // wide, :, lanes] = factors(shape_ref[part], rate_ref[part])
        for r in range(j * each, (j + 1) * each):
            sent_ref[r] = total[r, sent, :].astype(bf16)
            if r < near:
                kept_ref[r] = total[r, kept, :].astype(bf16)
    out.wait()


def pair_clicks(tile_rows, tile_cols, tile_count, clicks, item_shape, item_rate, blocks):
    slots, edge, _ = clicks.shape
    items, comps = item_shape.shape
    half = edge // 2
    vmem, hbm = pl.BlockSpec(memory_space=pltpu.VMEM), pl.BlockSpec(memory_space=pltpu.HBM)
    return pl.pallas_call(
        functools.partial(add_clicks, slots, edge),
        out_shape=(
            pltpu.VMEM((blocks - FAR, half, items), bf16),
            pltpu.HBM((FAR, half, items), bf16),
            pltpu.VMEM((blocks + comps // half, half, items), bf16),
        ),
        in_specs=[hbm] * 6,
        out_specs=(vmem, hbm, vmem),
        scratch_shapes=[
            pltpu.VMEM((blocks + 1, edge, items), f32),
            pltpu.VMEM((slots, edge, edge), bf16),
            pltpu.VMEM((FAR, half, items), bf16),
            pltpu.SMEM(tile_rows.shape, jnp.int32),
            pltpu.SMEM(tile_cols.shape, jnp.int32),
            pltpu.SMEM(tile_count.shape, jnp.int32),
            pltpu.VMEM(item_shape.shape, f32),
            pltpu.VMEM(item_rate.shape, f32),
            pltpu.SemaphoreType.DMA((slots // CHUNK + 1,)),
            pltpu.SemaphoreType.DMA((5,)),
        ],
        compiler_params=pltpu.CompilerParams(vmem_limit_bytes=56 << 20),
        cost_estimate=pl.CostEstimate(flops=slots * edge * edge, bytes_accessed=2 * slots * edge * edge, transcendentals=0),
        name="pair_clicks",
    )(tile_rows, tile_cols, tile_count, clicks, item_shape, item_rate)


def sent_factors(sent_ref, blocks, comps):
    return jnp.concatenate(
        [sent_ref[q, :, j : j + comps] for q in range(blocks, sent_ref.shape[0]) for j in range(0, sent_ref.shape[2], comps)],
        0,
    )


def add_terms(a_ref, cuts, counts_of, b, add_users, total):
    _, half, comps = a_ref.shape
    total[...] = jnp.zeros_like(total)
    for first, last in zip(cuts, cuts[1:]):
        at = pl.ds(first, last - first)
        rows = (last - first) * half
        a = a_ref[at].reshape(rows, comps)
        denom = lax.dot_general(a, b, LANES, preferred_element_type=f32)
        ratio = (counts_of(first, last).reshape(rows, -1).astype(f32) / denom).astype(bf16)
        product = jnp.dot(ratio, b, preferred_element_type=f32)
        add_users(at, (a.astype(f32) * product).reshape(-1, half, comps))
        total[...] += lax.dot_general(a, ratio, ROWS, preferred_element_type=f32)


def place_items(b, sums, out_ref, part, items_of):
    blocks = out_ref.shape[0]
    terms = (b.astype(f32) * sums.T).reshape(blocks, items_of, -1)
    out_ref[:, pl.ds(pl.multiple_of(part * items_of, items_of), items_of), :] = terms


def own_items(a_ref, sent_ref, kept_ref, tail_ref, user_ref, item_ref, same_ref, total, held, sem):
    blocks, _, comps = a_ref.shape
    copy = pltpu.make_async_copy(tail_ref, held, sem)
    copy.start()
    b = sent_factors(sent_ref, blocks, comps)

    near = kept_ref.shape[0]

    def counts_of(first, last):
        if last <= near:
            return kept_ref[first:last]
        copy.wait()
        return held[...]

    def add_users(at, terms):
        user_ref[at] = terms

    add_terms(a_ref, (0, near // 2, near, blocks), counts_of, b, add_users, total)
    place_items(b, total[...], item_ref, this_core(), b.shape[0] // blocks)


def near_items(a, sent, kept, tail):
    vmem, hbm = pl.BlockSpec(memory_space=pltpu.VMEM), pl.BlockSpec(memory_space=pltpu.HBM)
    items = sent.shape[2]
    users, item_sums, _ = pl.pallas_call(
        own_items,
        out_shape=(pltpu.VMEM(a.shape, f32), pltpu.VMEM(a.shape, f32), pltpu.HBM(tail.shape, bf16)),
        in_specs=[vmem, vmem, vmem, hbm],
        out_specs=(vmem, vmem, hbm),
        scratch_shapes=[pltpu.VMEM((a.shape[2], items), f32), pltpu.VMEM(tail.shape, bf16), pltpu.SemaphoreType.DMA],
        input_output_aliases={3: 2},
        compiler_params=pltpu.CompilerParams(vmem_limit_bytes=24 << 20),
        cost_estimate=pl.CostEstimate(flops=1 << 34, bytes_accessed=1 << 24, transcendentals=0),
        name="own_items",
    )(a, sent, kept, tail)
    return users, item_sums


def other_items(a_ref, got_ref, user_ref, item_ref, keep_ref, send_ref, total, users, items):
    core = this_core()
    blocks, half, comps = a_ref.shape
    b = sent_factors(got_ref, blocks, comps)

    def counts_of(first, last):
        return got_ref[first:last]

    def add_users(at, terms):
        users[at] = user_ref[at] + terms

    add_terms(a_ref, (0, blocks // 2, blocks), counts_of, b, add_users, total)
    rows = b.shape[0] // blocks
    items[...] = item_ref[...]
    place_items(b, total[...], items, 1 - core, rows)

    @pl.when(core == 0)
    def _():
        keep_ref[...] = users[...]
        send_ref[...] = items[...].astype(bf16)

    @pl.when(core != 0)
    def _():
        keep_ref[...] = items[...]
        send_ref[...] = users[...].astype(bf16)


def first_terms(keep_ref, sent_ref, out_ref):
    other = jnp.where(this_core() == 0, 0.0, sent_ref[0].astype(f32))
    out_ref[...] = (keep_ref[...] + other).astype(bf16)


def second_terms(parts_ref, sent_ref, new_ref, out_ref):
    total = jnp.sum(parts_ref[...].astype(f32), 0)
    new_ref[...] = prior_shape + total

    @pl.when(this_core() == 0)
    def _():
        out_ref[...] = sent_ref[1]

    @pl.when(this_core() != 0)
    def _():
        out_ref[...] = jnp.broadcast_to(total.astype(bf16)[None], out_ref.shape)


def finish(new_ref, parts_ref, user_ref, item_ref):
    rows = parts_ref.shape[2] // 2

    @pl.when(this_core() == 0)
    def _():
        user_ref[...] = new_ref[...]
        item_ref[...] = prior_shape + parts_ref[1, :, :rows].astype(f32).reshape(item_ref.shape)

    @pl.when(this_core() != 0)
    def _():
        user_ref[...] = prior_shape + jnp.sum(parts_ref[0].astype(f32), 0)
        item_ref[...] = prior_shape + parts_ref[1, :, rows:].astype(f32).reshape(item_ref.shape)


def small(kernel, out_shape, *operands, scratch=(), limit=24):
    vmem = pl.BlockSpec(memory_space=pltpu.VMEM)
    return pl.pallas_call(
        kernel,
        out_shape=out_shape,
        in_specs=[vmem] * len(operands),
        out_specs=jax.tree.map(lambda _: vmem, out_shape),
        scratch_shapes=list(scratch),
        compiler_params=pltpu.CompilerParams(vmem_limit_bytes=limit << 20),
        name=kernel.__name__,
    )(*operands)


def body(n_group, n_shard, user_shape, user_rate, item_shape, item_rate, tile_rows, tile_cols, clicks, tile_count):
    own, comps = user_shape.shape
    items = item_shape.shape[0]
    edge = clicks.shape[1]
    chips = n_shard // 2
    both = ("group", "shard")
    swap = [(s, s ^ 1) for s in range(n_shard)]
    pairs = [[2 * r, 2 * r + 1] for r in range(chips)]
    same_core = [[2 * r + c for r in range(chips)] for c in range(2)]
    users_or_items = [[g * n_shard + 2 * r for r in range(chips)] for g in range(n_group)]
    users_or_items += [[g * n_shard + 2 * r + 1 for g in range(n_group)] for r in range(chips)]

    copies = small(user_copies, jax.ShapeDtypeStruct((chips, own, comps), bf16), user_shape, user_rate, limit=56)
    a_mine = lax.all_to_all(copies, "shard", 0, 0, axis_index_groups=same_core)
    kept, tail, sent = pair_clicks(tile_rows, tile_cols, tile_count, clicks, item_shape, item_rate, chips)
    other = lax.ppermute(sent, "shard", swap)
    whole = (chips, own, comps)
    users, item_sums = near_items(a_mine, sent, kept, tail)
    keep, send = small(
        other_items, (pltpu.VMEM(whole, f32), pltpu.VMEM(whole, bf16)), a_mine, other, users, item_sums,
        scratch=(pltpu.VMEM((comps, items), f32), pltpu.VMEM(whole, f32), pltpu.VMEM(whole, f32)),
    )
    sent = lax.all_gather(send, "shard", axis_index_groups=pairs)
    terms = small(first_terms, jax.ShapeDtypeStruct(whole, bf16), keep, sent)
    parts = lax.all_to_all(terms, both, 0, 0, axis_index_groups=users_or_items)
    new, terms = small(
        second_terms, (jax.ShapeDtypeStruct((own, comps), f32), jax.ShapeDtypeStruct(whole, bf16)), parts, sent
    )
    parts = lax.all_to_all(terms, both, 0, 0, axis_index_groups=users_or_items)
    parts = lax.all_gather(parts, "shard", axis_index_groups=pairs)
    return small(
        finish, (jax.ShapeDtypeStruct((own, comps), f32), jax.ShapeDtypeStruct((items, comps), f32)), new, parts
    )


def solution(mesh):
    return jax.shard_map(
        functools.partial(body, mesh.shape["group"], mesh.shape["shard"]),
        mesh=mesh,
        in_specs=(
            P(("group", "shard"), None),
            P(("group", "shard"), None),
            P("shard", None),
            P("shard", None),
            P(("group", "shard")),
            P(("group", "shard")),
            P(("group", "shard"), None, None),
            P(("group", "shard")),
        ),
        out_specs=(P(("group", "shard"), None), P("shard", None)),
        check_vma=False,
    )
```
